32 devices in a mesh: dp: 8 (over y, x, core), tensor: 4 (over z).
Axes of the slice: x: 2, y: 2, z: 4, core: 2. Of those that a mesh axis runs over, the one named last changes fastest.
Arguments:
- activations: bfloat16 [2048, 8192], P('dp'), may hold values from -6 to 6
- out_grad: bfloat16 [2048, 2048], P('dp', 'tensor'), may hold values from -6 to 6
- weight: bfloat16 [8192, 2048], P(None, 'tensor'), may hold values from -0.0625 to 0.0625
- left_stats: float32 [8192, 2048], P('dp', 'tensor'), may hold values from -100 to 100, as said below
- right_stats: float32 [8192, 2048], P('dp', 'tensor'), may hold values from -100 to 100, as said below
Outputs:
- input_grad: bfloat16 [2048, 8192], P('dp', 'tensor')
- update: bfloat16 [8192, 2048], P('dp', 'tensor')
- left_new: float32 [8192, 2048], P('dp', 'tensor')
- right_new: float32 [8192, 2048], P('dp', 'tensor')
The draws below stay inside these ranges and needn't reach their ends.
Inputs may be any that keep to these rules, and one draw needn't show every extreme that they name: `left_stats`: every 512 x 512 block at rows i * 512 and columns j * 512 is symmetric and positive definite. `right_stats`: every 512 x 512 block at rows i * 512 and columns j * 512 is symmetric and positive definite.
All inputs are finite; a program needn't handle non-finite values.
Results may differ from the reference program's by a relative error of at most 0.001.
Values may be sent and summed in bfloat16 or wider, within the bound.
A program may use at most 128 MiB of HBM per device.

```python
import math
import jax
import jax.numpy as jnp
from jax import lax

D = 8192
F = 2048
BLOCK = 512
ITERS = 10
TOKENS = 2048


def draw_statistic(key):
    block_total = D // BLOCK * (F // BLOCK)
    first_key, second_key = jax.random.split(key, 2)
    factors = jax.random.truncated_normal(first_key, -3.0, 3.0, (block_total, BLOCK, BLOCK), jnp.float32)
    products = jnp.einsum('bik,bjk->bij', factors, factors) / BLOCK
    diagonal = jnp.exp(jax.random.uniform(second_key, (block_total, BLOCK), jnp.float32, math.log(0.1), 0.0))
    products = products + diagonal[:, :, None] * jnp.eye(BLOCK, dtype=jnp.float32)
    shaped = products.reshape(D // BLOCK, F // BLOCK, BLOCK, BLOCK)
    return shaped.transpose(0, 2, 1, 3).reshape(D, F)


def draw_left_stats(key, part):
    return draw_statistic(jax.random.fold_in(key, 11))


def draw_right_stats(key, part):
    return draw_statistic(jax.random.fold_in(key, 23))


def with_spikes(values, rng, source, target, parts, factor):
    def block_of(dim):
        return (jnp.arange(values.shape[dim]) // (values.shape[dim] // parts)).reshape((-1,) + (1,) * (values.ndim - 1 - dim))

    one_side = jax.random.permutation(rng, parts)[block_of(target)]
    second = (block_of(target) + parts // 2) % parts
    return jnp.where((block_of(source) == one_side) | (block_of(source) == second), factor * values, values)


def steps_of(stream_key, shape, pieces, low, top_value):
    loudness, own = 1.0, jax.random.fold_in(stream_key, 6)
    for dim, parts in pieces:
        steps = jnp.exp(jax.random.uniform(jax.random.fold_in(own, dim), (parts,), jnp.float32, low / len(pieces), top_value / len(pieces)))
        loudness = loudness * jnp.repeat(steps, shape[dim] // parts).reshape([-1 if axis == dim else 1 for axis in range(len(shape))])
    return loudness


def normal_values(key, extent, width, bound, cuts=(), held_as=jnp.bfloat16):
    factor_of = steps_of(key, extent, cuts, -0.22, 0.18) if cuts else 1.0
    values = jax.random.normal(key, extent, jnp.float32) * width * factor_of
    return jnp.minimum(jnp.maximum(values, -bound), bound).astype(held_as)


def heavy_noise(rng, shape, width, most, pieces, heavy, kind=jnp.bfloat16):
    array = width * jax.random.normal(rng, shape, jnp.float32)
    if pieces:
        array = array * steps_of(rng, shape, pieces, -0.22, 0.18)
    return jnp.clip(with_spikes(array, jax.random.fold_in(rng, 3), *heavy), -most, most).astype(kind)


def setup_inputs(seed: int = 0) -> dict:
    keys = jax.random.split(jax.random.key(seed), 6)
    activations = heavy_noise(keys[0], (TOKENS, D), 1.0, 6.0, ((0, 8),), (0, 1, 8, 2.0))
    out_grad = normal_values(keys[1], (TOKENS, F), 1.0, 6.0, ((0, 8), (1, 4)))
    weight = normal_values(keys[2], (D, F), D ** -0.5, 0.0625, ((1, 4),))
    left_stats = draw_left_stats(jax.random.fold_in(keys[5], 71), 0)
    right_stats = draw_right_stats(jax.random.fold_in(keys[5], 71), 0)
    return {"activations": activations, "out_grad": out_grad, "weight": weight, "left_stats": left_stats, "right_stats": right_stats}


decay_rate = 0.9

def batch_product(form, first, second):
    return jnp.einsum(form, first, second, precision=lax.Precision.HIGHEST)

def inverse_root(matrix):
    identity = jnp.eye(matrix.shape[-1], dtype=matrix.dtype)
    frobenius = jnp.sqrt(lax.optimization_barrier(jnp.sum(matrix * matrix, axis=(1, 2), keepdims=True)))
    current = matrix / frobenius
    result = jnp.broadcast_to(identity, matrix.shape)
    for iteration in range(ITERS):
        factor = (5.0 * identity - current) / 4.0
        result = batch_product('bij,bjk->bik', result, factor)
        squared = batch_product('bij,bjk->bik', factor, factor)
        fourth = batch_product('bij,bjk->bik', squared, squared)
        current = batch_product('bij,bjk->bik', fourth, current)
    return result / jnp.sqrt(jnp.sqrt(frobenius))

def split_blocks(whole_rows):
    row_total, col_total = whole_rows.shape
    shaped = whole_rows.reshape(row_total // BLOCK, BLOCK, col_total // BLOCK, BLOCK)
    return shaped.transpose(0, 2, 1, 3).reshape(-1, BLOCK, BLOCK)

def join_blocks(blocks, row_total, col_total):
    shaped = blocks.reshape(row_total // BLOCK, col_total // BLOCK, BLOCK, BLOCK)
    return shaped.transpose(0, 2, 1, 3).reshape(row_total, col_total)

def reference(activations, out_grad, weight, left_stats, right_stats):
    weight_grad = jnp.dot(activations.T, out_grad, preferred_element_type=jnp.float32) * TOKENS ** (-0.5)
    input_grad = jnp.dot(out_grad, weight.T, preferred_element_type=jnp.float32).astype(jnp.bfloat16)
    grad_blocks = split_blocks(weight_grad)
    left_gram = decay_rate * split_blocks(left_stats) + batch_product('bik,bjk->bij', grad_blocks, grad_blocks) / BLOCK
    right_gram = decay_rate * split_blocks(right_stats) + batch_product('bki,bkj->bij', grad_blocks, grad_blocks) / BLOCK
    block_total = grad_blocks.shape[0]
    roots = inverse_root(jnp.concatenate([left_gram, right_gram], 0))
    left_root = roots[:block_total]
    right_root = roots[block_total:]
    update = batch_product('bij,bjk->bik', batch_product('bij,bjk->bik', left_root, grad_blocks), right_root)
    update = join_blocks(update, D, F).astype(jnp.bfloat16)
    return (input_grad, update, join_blocks(left_gram, D, F), join_blocks(right_gram, D, F))
```

```python
import functools
import jax
import jax.numpy as jnp
from jax import lax
from jax.experimental import pallas as pl
from jax.experimental.pallas import tpu as pltpu
from jax.sharding import PartitionSpec as P

BLOCK = 512
ITERS = 10


decay_rate = 0.9


def from_partner(value, axis, apart):
    mask = 2**apart
    pairs = [(source, source ^ mask) for source in range(lax.axis_size(axis))]
    return lax.ppermute(value, axis, pairs)


def batch_product(form, first, second):
    return jnp.einsum(form, first, second, precision=lax.Precision.HIGH)


def parts(value):
    high = value.astype(jnp.bfloat16)
    return high, (value - high.astype(jnp.float32)).astype(jnp.bfloat16)


def product(first, second):
    (first_high, first_low), (second_high, second_low) = first, second
    return jnp.dot(
        jnp.concatenate([first_high, first_high, first_low], 1),
        jnp.concatenate([second_high, second_low, second_high], 0),
        preferred_element_type=jnp.float32,
    )


def root_kernel(count, *refs):
    ins, outs = refs[:count], refs[count : 2 * count]
    current_ref, result_ref = refs[2 * count :]
    order = ins[0].shape[-1]
    row = lax.broadcasted_iota(jnp.int32, (order, order), 0)
    col = lax.broadcasted_iota(jnp.int32, (order, order), 1)
    identity = (row == col).astype(jnp.float32)
    norms = []
    for place in range(count):
        matrix = ins[place][0]
        column_sums = jnp.sum(matrix * matrix, axis=0, keepdims=True)
        norms.append(jnp.sqrt(jnp.sum(column_sums, axis=1, keepdims=True)))
        current = matrix / norms[place]
        current_ref[place] = current
        result_ref[place] = (5.0 * identity - current) * 0.25

    def step(_, carry):
        for place in range(count):
            current = current_ref[place]
            first = parts(current)
            square = product(first, first)
            square_parts = parts(square)
            cube = product(square_parts, first)
            tail = product(square_parts, parts(cube - 20.0 * square))
            current = (625.0 * current - 500.0 * square + 150.0 * cube + tail) * (1.0 / 256.0)
            current_ref[place] = current
            result = result_ref[place]
            result_ref[place] = result + product(parts(result), parts((identity - current) * 0.25))
        return carry

    lax.fori_loop(0, ITERS - 1, step, 0)
    for place in range(count):
        outs[place][0] = result_ref[place] / jnp.sqrt(jnp.sqrt(norms[place]))


def inverse_roots(*matrices):
    count = len(matrices)
    total, order, _ = matrices[0].shape
    spec = pl.BlockSpec((1, order, order), lambda i: (i, 0, 0))
    return pl.pallas_call(
        functools.partial(root_kernel, count),
        grid=(total,),
        in_specs=[spec] * count,
        out_specs=[spec] * count,
        out_shape=[jax.ShapeDtypeStruct(m.shape, jnp.float32) for m in matrices],
        scratch_shapes=[pltpu.VMEM((count, order, order), jnp.float32)] * 2,
        compiler_params=pltpu.CompilerParams(vmem_limit_bytes=40 * 2**20),
        cost_estimate=pl.CostEstimate(
            flops=24 * count * total * (ITERS - 1) * order**3,
            bytes_accessed=8 * count * total * order**2,
            transcendentals=0,
        ),
    )(*matrices)


def split_blocks(whole_rows):
    row_total, col_total = whole_rows.shape
    shaped = whole_rows.reshape(row_total // BLOCK, BLOCK, col_total // BLOCK, BLOCK)
    return shaped.transpose(0, 2, 1, 3).reshape(-1, BLOCK, BLOCK)


def join_blocks(blocks, row_total, col_total):
    shaped = blocks.reshape(row_total // BLOCK, col_total // BLOCK, BLOCK, BLOCK)
    return shaped.transpose(0, 2, 1, 3).reshape(row_total, col_total)


def precondition(grad_rows, left_stats, right_stats):
    rows_local, cols_local = left_stats.shape
    dp_index = lax.axis_index("dp")
    paired = rows_local < BLOCK
    if paired:
        lower_half = dp_index % 2 == 0
        partner_pieces = from_partner((grad_rows, left_stats, right_stats), "dp", 0)

        def attach(own_part, peer_part):
            return jnp.where(
                lower_half,
                jnp.concatenate([own_part, peer_part], 0),
                jnp.concatenate([peer_part, own_part], 0),
            )

        grad_full = attach(grad_rows, partner_pieces[0])
        left_full = attach(left_stats, partner_pieces[1])
        right_full = attach(right_stats, partner_pieces[2])
    else:
        grad_full, left_full, right_full = (grad_rows, left_stats, right_stats)
    grad_blocks = split_blocks(grad_full)
    left_gram = (
        decay_rate * split_blocks(left_full)
        + batch_product("bik,bjk->bij", grad_blocks, grad_blocks) / BLOCK
    )
    right_gram = (
        decay_rate * split_blocks(right_full)
        + batch_product("bki,bkj->bij", grad_blocks, grad_blocks) / BLOCK
    )
    if paired:
        own_stat = jnp.where(lower_half, left_gram, right_gram)
        (own_root,) = inverse_roots(own_stat)
        partner_root = from_partner(own_root, "dp", 0)
        left_root = jnp.where(lower_half, own_root, partner_root)
        right_root = jnp.where(lower_half, partner_root, own_root)
    else:
        left_root, right_root = inverse_roots(left_gram, right_gram)
    update = batch_product(
        "bij,bjk->bik", batch_product("bij,bjk->bik", left_root, grad_blocks), right_root
    )
    row_total = grad_full.shape[0]
    update_rows = join_blocks(update, row_total, cols_local)
    left_rows = join_blocks(left_gram, row_total, cols_local)
    right_rows = join_blocks(right_gram, row_total, cols_local)
    if paired:
        offset = dp_index % 2 * rows_local
        update_rows = lax.dynamic_slice_in_dim(update_rows, offset, rows_local, 0)
        left_rows = lax.dynamic_slice_in_dim(left_rows, offset, rows_local, 0)
        right_rows = lax.dynamic_slice_in_dim(right_rows, offset, rows_local, 0)
    return (update_rows.astype(jnp.bfloat16), left_rows, right_rows)


def shards(activations, out_grad, weight, left_stats, right_stats):
    rows_local, cols_local = left_stats.shape
    dp_total = lax.axis_size("dp")
    tokens_local = activations.shape[0]
    scale = (tokens_local * dp_total) ** (-0.5)
    chunk_rows = min(rows_local, BLOCK)
    chunks = rows_local // chunk_rows
    pieces = activations.reshape(tokens_local, dp_total, chunks, chunk_rows)
    grads = lax.all_gather(out_grad, "dp", axis=0, tiled=True)
    spreads = [
        lax.all_to_all(
            pieces[:, :, chunk].reshape(tokens_local, dp_total * chunk_rows),
            "dp",
            split_axis=1,
            concat_axis=0,
            tiled=True,
        )
        for chunk in range(chunks)
    ]
    partial_terms = lax.dot_general(
        out_grad, weight, (((1,), (1,)), ((), ())), preferred_element_type=jnp.float32
    )
    input_grad = lax.psum_scatter(partial_terms, "tensor", scatter_dimension=1, tiled=True).astype(
        jnp.bfloat16
    )
    outs = []
    for chunk in range(chunks):
        summed = lax.dot_general(
            spreads[chunk], grads, (((0,), (0,)), ((), ())), preferred_element_type=jnp.float32
        )
        rows = slice(chunk * chunk_rows, (chunk + 1) * chunk_rows)
        outs.append(precondition(summed * scale, left_stats[rows], right_stats[rows]))
    joined = [jnp.concatenate(group, 0) for group in zip(*outs)]
    return (input_grad, *joined)


def solution(mesh):
    placed = (
        P("dp", None),
        P("dp", "tensor"),
        P(None, "tensor"),
        P("dp", "tensor"),
        P("dp", "tensor"),
    )
    return jax.shard_map(
        shards,
        mesh=mesh,
        in_specs=placed,
        out_specs=(P("dp", "tensor"), P("dp", "tensor"), P("dp", "tensor"), P("dp", "tensor")),
        check_vma=False,
    )
```
